128 devices in a mesh: row: 16 (over z_hi, x, core), col: 8 (over y, z_lo).
Axes of the slice: x: 4, y: 4, z: 4 (z_hi: 2, z_lo: 2; z = z_hi * 2 + z_lo), core: 2. Of those that a mesh axis runs over, the one named last changes fastest.
Arguments:
- node_features: bfloat16 [8, 16, 1024, 256], P('col', 'row'), may hold values from -6 to 6
- weight: bfloat16 [256, 256], replicated, may hold values from -0.375 to 0.375
- bias: float32 [256], replicated, may hold values from -4 to 4
- adj_blocks: bfloat16 [16, 8, 192, 128, 128], P('row', 'col'), may hold values from -0.15625 to 0.15625
- block_row: int32 [16, 8, 192], P('row', 'col'), may hold values from 0 to 63, as said below
- block_col: int32 [16, 8, 192], P('row', 'col'), may hold values from 0 to 127
- slot_count: int32 [16, 8], P('row', 'col'), may hold values from 48 to 192, as said below
- cotangent: bfloat16 [16, 8, 1024, 256], P('row', 'col'), may hold values from -6 to 6
Outputs:
- layer_out: bfloat16 [16, 8, 1024, 256], P('row', 'col')
- grad_input: bfloat16 [8, 16, 1024, 256], P('col', 'row')
- grad_weight: float32 [256, 256], replicated
- grad_bias: float32 [256], replicated
The draws below stay inside these ranges and needn't reach their ends.
Inputs may be any that keep to these rules, and one draw needn't show every extreme that they name: Within one grid cell the pairs (block_row, block_col) of all 192 slots are distinct; block_row lies in 0 to 63. `slot_count`: each cell holds 192, 96, 64 or 48 live slots; some cell holds 192 in every draw.
All inputs are finite; a program needn't handle non-finite values.
Results may differ from the reference program's by a relative error of at most 0.022.
Values may be sent and summed in bfloat16 or wider, within the bound.
No kernel may reach another device: no remote copies, remote signals or barrier semaphores. Data moves between devices by JAX's collectives and lax.ppermute only.
A program may use at most 128 MiB of HBM per device.

```python
import jax
import jax.numpy as jnp
from jax import lax

F = 256
BLK = 128
SLOTS = 192
NPD = 1024
RB = 64
CB = 128
NODES = 131072
N_ROW = 16
N_COL = 8


def pattern(key):
    device_keys = jax.random.split(key, N_ROW * N_COL)
    orders = jax.vmap(lambda single: jax.random.permutation(single, RB * CB))(device_keys)
    picked = orders[:, :SLOTS].astype(jnp.int32)
    return picked.reshape(N_ROW, N_COL, SLOTS)


def draw_block_row(key, part):
    picked = pattern(key)
    return (picked // CB).astype(jnp.int32)


def draw_block_col(key, part):
    picked = pattern(key)
    return (picked % CB).astype(jnp.int32)


def draw_slot_count(key, part):
    key = jax.random.fold_in(key, 3)
    first_key, second_key = jax.random.split(key)
    levels = jax.random.randint(first_key, (N_ROW * N_COL,), 1, 5)
    counts = (SLOTS // levels).astype(jnp.int32)
    chosen = jax.random.randint(second_key, (), 0, N_ROW * N_COL)
    flattened = jnp.where(jnp.arange(N_ROW * N_COL) == chosen, SLOTS, counts)
    return flattened.reshape(N_ROW, N_COL).astype(jnp.int32)


def level_of(key, shape, cuts, smallest, high):
    factor_of = 1.0
    for axis_at, blocks in cuts:
        steps = jax.random.uniform(jax.random.fold_in(jax.random.fold_in(key, 6), axis_at), (blocks,), jnp.float32, smallest / len(cuts), high / len(cuts))
        factor_of = factor_of * jnp.repeat(jnp.exp(steps), shape[axis_at] // blocks).reshape((-1,) + (1,) * (len(shape) - 1 - axis_at))
    return factor_of


def gaussian(stream_key, shape, deviation, limit, pieces=(), dtype=jnp.bfloat16):
    drawn = deviation * jax.random.normal(stream_key, shape, jnp.float32)
    if pieces:
        drawn = drawn * level_of(stream_key, shape, pieces, -0.22, 0.18)
    return jnp.clip(drawn, -limit, limit).astype(dtype)


def setup_inputs(seed: int = 0) -> dict:
    streams_of = jax.random.split(jax.random.key(seed), 9)
    return {
        "node_features": gaussian(streams_of[0], (N_COL, N_ROW, NPD, F), 1.0, 6.0, ((0, 8), (1, 16))),
        "weight": gaussian(streams_of[1], (F, F), F ** -0.5, 0.375),
        "bias": gaussian(streams_of[2], (F,), 1.0, 4.0, (), jnp.float32),
        "adj_blocks": gaussian(streams_of[3], (N_ROW, N_COL, SLOTS, BLK, BLK), (12 * BLK) ** -0.5, 0.15625, ((0, 16), (1, 8))),
        "block_row": draw_block_row(jax.random.fold_in(streams_of[8], 71), 0),
        "block_col": draw_block_col(jax.random.fold_in(streams_of[8], 71), 0),
        "slot_count": draw_slot_count(jax.random.fold_in(streams_of[8], 71), 0),
        "cotangent": gaussian(streams_of[7], (N_ROW, N_COL, NPD, F), 1.0, 6.0, ((0, 16), (1, 8))),
    }


def cell_forward(blocks, row_ids, col_ids, count, table):
    size = blocks.shape[-1]
    width = table.shape[-1]
    picked = table.reshape(-1, size, width)[col_ids]
    contrib = jnp.einsum("sbk,skf->sbf", blocks.astype(jnp.float32), picked.astype(jnp.float32), precision=lax.Precision.HIGHEST)
    live_slots = jnp.arange(blocks.shape[0]) < count
    targets = jnp.where(live_slots, row_ids, RB).astype(jnp.int32)
    summed = jax.ops.segment_sum(contrib, targets, num_segments=RB + 1)[:RB]
    return summed.reshape(RB * size, width).astype(jnp.bfloat16)


def cell_backward(blocks, row_ids, col_ids, count, table):
    size = blocks.shape[-1]
    width = table.shape[-1]
    picked = table.reshape(-1, size, width)[row_ids]
    contrib = jnp.einsum("sbk,sbf->skf", blocks.astype(jnp.float32), picked.astype(jnp.float32), precision=lax.Precision.HIGHEST)
    live_slots = jnp.arange(blocks.shape[0]) < count
    targets = jnp.where(live_slots, col_ids, CB).astype(jnp.int32)
    summed = jax.ops.segment_sum(contrib, targets, num_segments=CB + 1)[:CB]
    return summed.reshape(CB * size, width).astype(jnp.bfloat16)


def reference(node_features, weight, bias, adj_blocks, block_row, block_col, slot_count, cotangent):
    flat_in = node_features.reshape(NODES, F)
    projected = jnp.dot(flat_in, weight, preferred_element_type=jnp.float32).astype(jnp.bfloat16)
    column_tables = projected.reshape(N_COL, CB * BLK, F)

    def one_row(items):
        blocks_r, rows_r, cols_r, count_r = items
        parts = lax.map(lambda inner: cell_forward(*inner), (blocks_r, rows_r, cols_r, count_r, column_tables))
        return jnp.sum(parts.astype(jnp.float32), axis=0)

    aggregate = lax.map(one_row, (adj_blocks, block_row, block_col, slot_count))
    pre = aggregate.reshape(N_ROW, N_COL, NPD, F) + bias
    layer_out = jax.nn.silu(pre).astype(jnp.bfloat16)
    sigma = jax.nn.sigmoid(pre)
    grad_pre = (cotangent.astype(jnp.float32) * sigma * (1.0 + pre * (1.0 - sigma))).astype(jnp.bfloat16)
    row_tables = grad_pre.reshape(N_ROW, RB * BLK, F)
    swapped = (jnp.swapaxes(adj_blocks, 0, 1), jnp.swapaxes(block_row, 0, 1), jnp.swapaxes(block_col, 0, 1), jnp.swapaxes(slot_count, 0, 1))

    def one_col(items):
        blocks_c, rows_c, cols_c, count_c = items
        parts = lax.map(lambda inner: cell_backward(*inner), (blocks_c, rows_c, cols_c, count_c, row_tables))
        return jnp.sum(parts.astype(jnp.float32), axis=0)

    grad_projected = lax.map(one_col, swapped).reshape(NODES, F).astype(jnp.bfloat16)
    grad_input = jnp.dot(grad_projected, weight.T, preferred_element_type=jnp.float32).astype(jnp.bfloat16)
    grad_weight = jnp.dot(flat_in.T, grad_projected, preferred_element_type=jnp.float32)
    grad_bias = jnp.sum(grad_pre.astype(jnp.float32).reshape(NODES, F), axis=0)
    return layer_out, grad_input.reshape(N_COL, N_ROW, NPD, F), grad_weight, grad_bias
```

```python
import functools

import jax
import jax.numpy as jnp
from jax import lax
from jax.experimental import pallas as pl
from jax.experimental.pallas import tpu as pltpu
from jax.sharding import PartitionSpec as P

BLK = 128
UNROLL = 8
CHUNK = 16


def row_index(zh, x, c):
    return zh * 8 + x * 2 + c


def row_perm(move):
    return [
        (row_index(zh, x, c), row_index(*move(zh, x, c)))
        for zh in range(2)
        for x in range(4)
        for c in range(2)
    ]


def col_perm(move):
    def index(zl, y):
        return y * 2 + zl

    return [(index(zl, y), index(*move(zl, y))) for zl in range(2) for y in range(4)]


ROW_RING = {d: row_perm(lambda zh, x, c, d=d: (zh, (x + d) % 4, c)) for d in (1, 2, 3)}
ROW_PAIR = row_perm(lambda zh, x, c: (1 - zh, x, c))
ROW_CORE = row_perm(lambda zh, x, c: (zh, x, 1 - c))
COL_RING = {d: col_perm(lambda zl, y, d=d: (zl, (y + d) % 4)) for d in (1, 2, 3)}
COL_PAIR = col_perm(lambda zl, y: (1 - zl, y))


def gather(own, axis, ring, pair):
    def go(v, perm):
        return lax.ppermute(v, axis, perm)

    got = {(0, 0): own}
    got[1, 0] = go(own, pair)
    got[0, 3] = go(own, ring[1])
    got[0, 1] = go(own, ring[3])
    got[0, 2] = go(own, ring[2])
    got[1, 3] = go(got[1, 0], ring[1])
    got[1, 1] = go(got[1, 0], ring[3])
    got[1, 2] = go(got[0, 2], pair)
    return got


def scatter(parts, axis, ring, pair):
    def go(v, perm):
        return lax.ppermute(v.astype(jnp.bfloat16), axis, perm).astype(jnp.float32)

    up = go(parts(1, 1), ring[1])
    down = go(parts(1, 3), ring[3])
    far = go(parts(1, 2), pair)
    up_own = go(parts(0, 1), ring[1])
    down_own = go(parts(0, 3), ring[3])
    across = go(parts(1, 0) + up + down, pair)
    far_own = go(parts(0, 2) + far, ring[2])
    return parts(0, 0) + up_own + down_own + across + far_own


def sparse_kernel(transpose, n_in, n_out, rows, cols, count, adj, *refs):
    pieces = refs[:n_in]
    outs = refs[n_in : n_in + n_out]
    table, acc, blocks, piece_sem, block_sem = refs[n_in + n_out :]
    n_slots = adj.shape[0]
    n_chunks = n_slots // CHUNK
    piece_rows = pieces[0].shape[0]
    piece_copies = [
        pltpu.make_async_copy(
            pieces[i], table.at[pl.ds(i * piece_rows, piece_rows)], piece_sem.at[i]
        )
        for i in range(n_in)
    ]
    block_copies = [
        pltpu.make_async_copy(
            adj.at[pl.ds(i * CHUNK, CHUNK)], blocks.at[pl.ds(i * CHUNK, CHUNK)], block_sem.at[i]
        )
        for i in range(n_chunks)
    ]
    for copy in piece_copies + block_copies:
        copy.start()
    live = count[0]

    @pl.loop(0, acc.shape[0] // 256)
    def _(i):
        acc[pl.ds(pl.multiple_of(i * 256, 256), 256), :] = jnp.zeros((256, acc.shape[1]), acc.dtype)

    for copy in piece_copies + block_copies:
        copy.wait()

    @pl.loop(0, live // UNROLL)
    def _(step):
        base = step * UNROLL
        for u in range(UNROLL):
            slot = base + u
            a = blocks[slot]
            out_at = pl.multiple_of(rows[slot] * BLK, BLK)
            in_at = pl.multiple_of(cols[slot] * BLK, BLK)
            t = table[pl.ds(in_at, BLK), :]
            dims = (((0,), (0,)), ((), ())) if transpose else (((1,), (0,)), ((), ()))
            prod = lax.dot_general(a, t, dims, preferred_element_type=jnp.float32)
            acc[pl.ds(out_at, BLK), :] += prod

    for i, out in enumerate(outs):

        @pl.loop(0, piece_rows // 128)
        def _(j):
            at = pl.multiple_of(j * 128, 128)
            out[pl.ds(at, 128), :] = acc[pl.ds(i * piece_rows + at, 128), :].astype(out.dtype)


def sparse(transpose, rows, cols, count, adj, pieces, n_out):
    n_in = len(pieces)
    piece_rows, width = pieces[0].shape
    n_slots = adj.shape[0]
    out_shape = [jax.ShapeDtypeStruct((piece_rows, width), jnp.bfloat16)] * n_out
    return pl.pallas_call(
        functools.partial(sparse_kernel, transpose, n_in, n_out),
        out_shape=out_shape,
        in_specs=[pl.BlockSpec(memory_space=pltpu.SMEM)] * 3
        + [pl.BlockSpec(memory_space=pl.ANY)] * (1 + n_in),
        out_specs=[pl.BlockSpec(memory_space=pltpu.VMEM)] * n_out,
        scratch_shapes=[
            pltpu.VMEM((n_in * piece_rows, width), jnp.bfloat16),
            pltpu.VMEM((n_out * piece_rows, width), jnp.float32),
            pltpu.VMEM((n_slots, BLK, BLK), jnp.bfloat16),
            pltpu.SemaphoreType.DMA((n_in,)),
            pltpu.SemaphoreType.DMA((n_slots // CHUNK,)),
        ],
        compiler_params=pltpu.CompilerParams(vmem_limit_bytes=48 * 1024 * 1024),
        cost_estimate=pl.CostEstimate(
            flops=2 * n_slots * BLK * BLK * width,
            bytes_accessed=n_slots * BLK * BLK * 2 + (n_in + n_out) * piece_rows * width * 2,
            transcendentals=0,
        ),
        name="sparse_back" if transpose else "sparse_forward",
    )(rows, cols, count, adj, *pieces)


def all_sum(v):
    half = v.shape[0] // 2
    core = lax.axis_index("row") % 2
    v = v + lax.ppermute(v, "row", ROW_CORE)
    part = lax.dynamic_slice_in_dim(v, core * half, half, 0)
    part = part + lax.ppermute(part, "row", ROW_PAIR)
    for bit in (1, 2):
        part = part + lax.ppermute(part, "row", row_perm(lambda zh, x, c: (zh, x ^ bit, c)))
    part = part + lax.ppermute(part, "col", COL_PAIR)
    for bit in (1, 2):
        part = part + lax.ppermute(part, "col", col_perm(lambda zl, y: (zl, y ^ bit)))
    other = lax.ppermute(part, "row", ROW_CORE)
    first = jnp.where(core == 0, part, other)
    second = jnp.where(core == 0, other, part)
    return jnp.concatenate([first, second], axis=0)


def local(node_features, weight, bias, adj_blocks, block_row, block_col, slot_count, cotangent):
    node_rows, width = node_features.shape[2:]
    per = node_rows // BLK
    adj = adj_blocks[0, 0]
    count = slot_count[0]
    me_row = lax.axis_index("row")
    me_col = lax.axis_index("col")
    zh, x, c = me_row // 8, (me_row // 2) % 4, me_row % 2
    y, zl = me_col // 2, me_col % 2

    owner = block_col[0, 0] // per
    rel_c = (owner % 2) ^ c
    rel_x = ((owner // 2) % 4 - x) % 4
    rel_zh = (owner // 8) ^ zh
    in_ids = (rel_c * 8 + rel_zh * 4 + rel_x) * per + block_col[0, 0] % per
    owner = block_row[0, 0] // per
    rel_zl = (owner % 2) ^ zl
    rel_y = (owner // 2 - y) % 4
    out_ids = (rel_zl * 4 + rel_y) * per + block_row[0, 0] % per

    own_input = node_features[0, 0]
    got = gather(own_input, "row", ROW_RING, ROW_PAIR)
    mine = [got[p, r] for p in range(2) for r in range(4)]
    swapped = {k: lax.ppermute(v, "row", ROW_CORE) for k, v in got.items()}
    theirs = [swapped[p, r] for p in range(2) for r in range(4)]
    sums = sparse(False, out_ids, in_ids, count, adj, mine + theirs, 8)
    aggregate = scatter(
        lambda p, r: sums[p * 4 + r].astype(jnp.float32), "col", COL_RING, COL_PAIR
    ).astype(jnp.bfloat16)

    pre = jnp.dot(aggregate, weight, preferred_element_type=jnp.float32) + bias
    sigma = jax.nn.sigmoid(pre)
    layer_out = (pre * sigma).astype(jnp.bfloat16)
    grad_pre = (cotangent[0, 0].astype(jnp.float32) * sigma * (1.0 + pre * (1.0 - sigma))).astype(
        jnp.bfloat16
    )

    got = gather(grad_pre, "col", COL_RING, COL_PAIR)
    pieces = [got[p, r] for p in range(2) for r in range(4)]
    weight_term = lax.dot_general(
        aggregate, grad_pre, (((0,), (0,)), ((), ())), preferred_element_type=jnp.float32
    )
    bias_term = jnp.sum(grad_pre.astype(jnp.float32), axis=0)
    both = jnp.concatenate(
        [weight_term, bias_term[None], jnp.zeros((15, width), jnp.float32)], axis=0
    )
    total = all_sum(both)

    backs = sparse(True, in_ids, out_ids, count, adj, pieces, 16)

    def summed(p, r):
        k = p * 4 + r
        other = lax.ppermute(backs[8 + k], "row", ROW_CORE)
        return backs[k].astype(jnp.float32) + other.astype(jnp.float32)

    grad_projected = scatter(summed, "row", ROW_RING, ROW_PAIR).astype(jnp.bfloat16)
    grad_input = lax.dot_general(
        grad_projected, weight, (((1,), (1,)), ((), ())), preferred_element_type=jnp.float32
    ).astype(jnp.bfloat16)
    return (
        layer_out.reshape(1, 1, node_rows, width),
        grad_input.reshape(1, 1, node_rows, width),
        total[:width],
        total[width],
    )


def solution(mesh):
    placed = (
        P("col", "row", None, None),
        P(),
        P(),
        P("row", "col", None, None, None),
        P("row", "col", None),
        P("row", "col", None),
        P("row", "col"),
        P("row", "col", None, None),
    )
    return jax.shard_map(
        local,
        mesh=mesh,
        in_specs=placed,
        out_specs=(P("row", "col", None, None), P("col", "row", None, None), P(), P()),
        check_vma=False,
    )
```

```python
import functools

import jax
import jax.numpy as jnp
from jax import lax
from jax.experimental import pallas as pl
from jax.experimental.pallas import tpu as pltpu
from jax.sharding import PartitionSpec as P

BLK = 128
UNROLL = 8
CHUNK = 16


def both_perms(move):
    row = [
        (p * 8 + r * 2 + c, q * 8 + s * 2 + d)
        for p in range(2)
        for r in range(4)
        for c in range(2)
        for q, s, d in [move(p, r, c)]
    ]
    col = [
        (((c * 4 + r) * 2 + p), ((d * 4 + s) * 2 + q))
        for p in range(2)
        for r in range(4)
        for c in range(2)
        for q, s, d in [move(p, r, c)]
    ]
    return row, col


def over(v, perm, kind):
    if kind == "row":
        return lax.ppermute(v, "row", perm[0])
    pairs = [
        ((high * 2 + a // 8) * 8 + a % 8, (high * 2 + b // 8) * 8 + b % 8)
        for high in range(8)
        for a, b in perm[1]
    ]
    return lax.ppermute(v, ("row", "col"), pairs)


PAIR = both_perms(lambda p, r, c: (1 - p, r, c))
CORE = both_perms(lambda p, r, c: (p, r, 1 - c))
OUT = both_perms(lambda p, r, c: (p, (r + 1 - 2 * c) % 4, c))
BACK = both_perms(lambda p, r, c: (p, (r - 1 + 2 * c) % 4, c))


def wide(v):
    return v.astype(jnp.float32)


def narrow(v):
    return v.astype(jnp.bfloat16)


def meet(*arrays):
    return lax.optimization_barrier(arrays)


def direct_side():
    return jnp.where(lax.axis_index("row") % 2 == 0, 3, 1)


def row_place(pair, ring, core):
    side = jnp.where(ring == direct_side(), 4 + pair * 2 + core, 9 + pair * 2 - core)
    return jnp.where(
        ring == 0, pair * 2 + core, jnp.where(ring == 2, 12 + core * 2 + pair, side)
    )


def col_place(pair, ring):
    side = jnp.where(ring == direct_side(), 2 + pair, 4 + pair)
    return jnp.where(ring == 0, pair, jnp.where(ring == 2, 6 + pair, side))


ROW_SIZES = (1, 1, 1, 1, 1, 1, 1, 1, 2, 2, 2, 2)


class Summer:
    def __init__(self, v):
        self.half = v.shape[0] // 2
        self.core = lax.axis_index("row") % 2
        self.part = v
        bits = [(p, b) for p in (0,) for b in (1, 2)]
        rings = [both_perms(lambda p, r, c, b=b: (p, r ^ b, c)) for _, b in bits]
        self.todo = [(CORE, "row"), (PAIR, "row"), (rings[0], "row"), (rings[1], "row")]
        self.todo += [(PAIR, "col"), (rings[0], "col"), (rings[1], "col")]
        self.got = over(v, *self.todo.pop(0))

    def step(self, *events):
        got, *events = meet(self.got, *events)
        self.part = self.part + got
        if len(self.todo) == 6:
            self.part = lax.dynamic_slice_in_dim(self.part, self.core * self.half, self.half, 0)
        if self.todo:
            self.got = over(self.part, *self.todo.pop(0))
        return events

    def result(self):
        other = over(self.part, CORE, "row")
        first = jnp.where(self.core == 0, self.part, other)
        second = jnp.where(self.core == 0, other, self.part)
        return jnp.concatenate([first, second], axis=0)


def gather(own, kind, extra=(), summer=None):
    step = (lambda *v: summer().step(*v)) if summer else meet
    far = over(own, PAIR, kind)
    near_a = over(own, OUT, kind)
    other = over(own, CORE, kind)
    near_b = over(other, OUT, kind)
    near_a, *extra = step(near_a, *extra)
    across = over(near_a, OUT, kind)
    near_b, far, _ = meet(near_b, far, near_a)
    far_other = over(far, CORE, kind)
    far_a = over(far, OUT, kind)
    far_b = over(far_other, OUT, kind)
    across, _ = step(across, far_other)
    across_far = over(across, PAIR, kind)
    near_b_swapped = over(near_b, CORE, kind)
    if kind == "row":
        near_a_swapped = over(near_a, CORE, kind)
        across_swapped = over(across, CORE, kind)
        far_a, _ = meet(far_a, across)
        far_a_swapped = over(far_a, CORE, kind)
    far_b, across_far = step(far_b, across_far)
    far_b_swapped = over(far_b, CORE, kind)
    if kind == "row":
        across_far_swapped = over(across_far, CORE, kind)
        pieces = [own, other, far, far_other, near_a, near_b, far_a, far_b]
        pieces += [near_a_swapped, near_b_swapped, far_a_swapped, far_b_swapped]
        pieces += [across, across_far, across_swapped, across_far_swapped]
    else:
        pieces = [own, far, near_a, far_a, near_b_swapped, far_b_swapped, across, across_far]
    return pieces, extra


def scatter(parts, kind, summer=None):
    step = (lambda *v: summer.step(*v)) if summer else meet
    parts = list(parts)
    if kind == "row":
        own, other, far, far_other, near_a, near_b, far_a, far_b = parts[:8]
        side_near, side_far, across, across_other = parts[8:]
        rows = own.shape[0]
        turned = over(across_other, CORE, kind)
        turned_far = over(side_far, CORE, kind)
        turned_near = over(side_near, CORE, kind)
        across_near = wide(across[:rows]) + wide(turned[:rows])
        across_far = narrow(wide(across[rows:]) + wide(turned[rows:]))
        far_a = narrow(wide(far_a) + wide(turned_far[:rows]))
        far_b = narrow(wide(far_b) + wide(turned_far[rows:]))
        near_a = wide(near_a) + wide(turned_near[:rows])
        near_b = narrow(wide(near_b) + wide(turned_near[rows:]))
    else:
        own, far, near_a, far_a, side_near, side_far, across_near, across_far = parts
        far_b = over(side_far, CORE, kind)
        near_b = over(side_near, CORE, kind)
        across_near, near_a = wide(across_near), wide(near_a)
        other = far_other = None

    def plus(v, w):
        return w if v is None else narrow(wide(v) + wide(w))

    got_far_b = over(far_b, BACK, kind)
    passed_far = over(across_far, PAIR, kind)
    got_far_a = over(far_a, BACK, kind)
    (got_far_b,) = step(got_far_b)
    core_far = over(plus(far_other, got_far_b), CORE, kind)
    passed_far, _ = step(passed_far, got_far_b)
    across_sum = narrow(across_near + wide(passed_far))
    passed = over(across_sum, BACK, kind)
    near_b, got_far_a, _ = meet(near_b, got_far_a, across_sum)
    got_near_b = over(near_b, BACK, kind)
    far_sum = narrow(wide(far) + wide(got_far_a) + wide(core_far))
    back_far = over(far_sum, PAIR, kind)
    passed, _ = step(passed, far_sum)
    got_near_a = over(narrow(near_a + wide(passed)), BACK, kind)
    got_near_b, _ = step(got_near_b, passed)
    core_near = over(plus(other, got_near_b), CORE, kind)
    got_near_a, back_far, core_near = meet(got_near_a, back_far, core_near)
    return wide(own) + wide(got_near_a) + wide(back_far) + wide(core_near)


def sparse_kernel(transpose, n_in, rows, cols, count, adj, *refs):
    pieces = refs[:n_in]
    outs = refs[n_in:-5]
    table, acc, blocks, piece_sem, block_sem = refs[-5:]
    piece_copies = []
    at = 0
    for i, piece in enumerate(pieces):
        part = table.at[pl.ds(at, piece.shape[0])]
        piece_copies.append(pltpu.make_async_copy(piece, part, piece_sem.at[i]))
        at += piece.shape[0]
    for copy in piece_copies:
        copy.start()
    n_chunks = count[0] // CHUNK

    def block_copy(i):
        part = pl.ds(i * CHUNK, CHUNK)
        return pltpu.make_async_copy(adj.at[part], blocks.at[part], block_sem.at[i])

    @pl.loop(0, n_chunks)
    def _(i):
        block_copy(i).start()

    @pl.loop(0, acc.shape[0] // 256)
    def _(i):
        acc[pl.ds(pl.multiple_of(i * 256, 256), 256), :] = jnp.zeros((256, acc.shape[1]), acc.dtype)

    for copy in piece_copies:
        copy.wait()

    @pl.loop(0, n_chunks)
    def _(i):
        block_copy(i).wait()

        @pl.loop(0, CHUNK // UNROLL)
        def _(step):
            for u in range(UNROLL):
                slot = i * CHUNK + step * UNROLL + u
                out_at = pl.multiple_of(rows[slot] * BLK, BLK)
                in_at = pl.multiple_of(cols[slot] * BLK, BLK)
                dims = (((0,), (0,)), ((), ())) if transpose else (((1,), (0,)), ((), ()))
                acc[pl.ds(out_at, BLK), :] += lax.dot_general(
                    blocks[slot],
                    table[pl.ds(in_at, BLK), :],
                    dims,
                    preferred_element_type=jnp.float32,
                )

    at = 0
    for out in outs:

        @pl.loop(0, out.shape[0] // BLK)
        def _(j, at=at, out=out):
            here = pl.multiple_of(j * BLK, BLK)
            out[pl.ds(here, BLK), :] = acc[pl.ds(at + here, BLK), :].astype(out.dtype)

        at += out.shape[0]


def sparse(transpose, rows, cols, count, adj, pieces, sizes):
    n_in = len(pieces)
    width = pieces[0].shape[1]
    in_rows = sum(piece.shape[0] for piece in pieces)
    n_slots = adj.shape[0]
    return pl.pallas_call(
        functools.partial(sparse_kernel, transpose, n_in),
        out_shape=[jax.ShapeDtypeStruct((size, width), jnp.bfloat16) for size in sizes],
        in_specs=[pl.BlockSpec(memory_space=pltpu.SMEM)] * 3
        + [pl.BlockSpec(memory_space=pltpu.HBM)]
        + [pl.BlockSpec(memory_space=pl.ANY)] * n_in,
        out_specs=[pl.BlockSpec(memory_space=pltpu.VMEM)] * len(sizes),
        scratch_shapes=[
            pltpu.VMEM((in_rows, width), jnp.bfloat16),
            pltpu.VMEM((sum(sizes), width), jnp.float32),
            pltpu.VMEM((n_slots, BLK, BLK), jnp.bfloat16),
            pltpu.SemaphoreType.DMA((n_in,)),
            pltpu.SemaphoreType.DMA((n_slots // CHUNK,)),
        ],
        compiler_params=pltpu.CompilerParams(vmem_limit_bytes=(38 if transpose else 30) * 1024 * 1024),
        cost_estimate=pl.CostEstimate(
            flops=2 * n_slots * BLK * BLK * width,
            bytes_accessed=n_slots * BLK * BLK * 2 + (in_rows + sum(sizes)) * width * 2,
            transcendentals=0,
        ),
        name="sparse_back" if transpose else "sparse_forward",
    )(rows, cols, count, adj, *pieces)


def local(node_features, weight, bias, adj_blocks, block_row, block_col, slot_count, cotangent):
    node_rows, width = node_features.shape[2:]
    per = node_rows // BLK
    adj = adj_blocks[0, 0]
    count = slot_count[0]
    me_row = lax.axis_index("row")
    me_col = lax.axis_index("col")

    owner = block_col[0, 0] // per
    place = row_place(
        (owner // 8) ^ (me_row // 8), (owner // 2 - me_row // 2) % 4, (owner ^ me_row) % 2
    )
    in_ids = place * per + block_col[0, 0] % per
    owner = block_row[0, 0] // per
    place = col_place((owner ^ me_col) % 2, (owner // 2 - me_col // 2) % 4)
    out_ids = place * per + block_row[0, 0] % per

    pieces, (in_ids, out_ids) = gather(node_features[0, 0], "row", (in_ids, out_ids))
    sums = sparse(False, out_ids, in_ids, count, adj, pieces, [node_rows] * 8)
    aggregate = narrow(scatter(sums, "col"))

    pre = jnp.dot(aggregate, weight, preferred_element_type=jnp.float32) + bias
    sigma = jax.nn.sigmoid(pre)
    layer_out = narrow(pre * sigma)
    grad_pre = narrow(wide(cotangent[0, 0]) * sigma * (1.0 + pre * (1.0 - sigma)))

    made = []

    def summer():
        if not made:
            weight_term = lax.dot_general(
                aggregate, grad_pre, (((0,), (0,)), ((), ())), preferred_element_type=jnp.float32
            )
            bias_term = jnp.sum(wide(grad_pre), axis=0)
            spare = jnp.zeros((15, width), jnp.float32)
            made.append(Summer(jnp.concatenate([weight_term, bias_term[None], spare], axis=0)))
        return made[0]

    pieces, _ = gather(grad_pre, "col", (), summer)
    backs = sparse(
        True, in_ids, out_ids, count, adj, pieces, [node_rows * size for size in ROW_SIZES]
    )
    grad_projected = narrow(scatter(backs, "row", summer()))
    grad_input = narrow(
        lax.dot_general(
            grad_projected, weight, (((1,), (1,)), ((), ())), preferred_element_type=jnp.float32
        )
    )
    summed = summer().result()
    return (
        layer_out.reshape(1, 1, node_rows, width),
        grad_input.reshape(1, 1, node_rows, width),
        summed[:width],
        summed[width],
    )


def solution(mesh):
    placed = (
        P("col", "row", None, None),
        P(),
        P(),
        P("row", "col", None, None, None),
        P("row", "col", None),
        P("row", "col", None),
        P("row", "col"),
        P("row", "col", None, None),
    )
    return jax.shard_map(
        local,
        mesh=mesh,
        in_specs=placed,
        out_specs=(P("row", "col", None, None), P("col", "row", None, None), P(), P()),
        check_vma=False,
    )
```

```python
import functools

import jax
import jax.numpy as jnp
from jax import lax
from jax.experimental import pallas as pl
from jax.experimental.pallas import tpu as pltpu
from jax.sharding import PartitionSpec as P

BLK = 128
CHUNK = 16
LONG = 3


def both_perms(move):
    row = [
        (p * 8 + r * 2 + c, q * 8 + s * 2 + d)
        for p in range(2)
        for r in range(4)
        for c in range(2)
        for q, s, d in [move(p, r, c)]
    ]
    col = [
        (((c * 4 + r) * 2 + p), ((d * 4 + s) * 2 + q))
        for p in range(2)
        for r in range(4)
        for c in range(2)
        for q, s, d in [move(p, r, c)]
    ]
    return row, col


def over(v, perm, kind):
    if kind == "row":
        return lax.ppermute(v, "row", perm[0])
    pairs = [
        ((high * 2 + a // 8) * 8 + a % 8, (high * 2 + b // 8) * 8 + b % 8)
        for high in range(8)
        for a, b in perm[1]
    ]
    return lax.ppermute(v, ("row", "col"), pairs)


PAIR = both_perms(lambda p, r, c: (1 - p, r, c))
CORE = both_perms(lambda p, r, c: (p, r, 1 - c))
OUT = both_perms(lambda p, r, c: (p, (r + 1 - 2 * c) % 4, c))
BACK = both_perms(lambda p, r, c: (p, (r - 1 + 2 * c) % 4, c))


def wide(v):
    return v.astype(jnp.float32)


def narrow(v):
    return v.astype(jnp.bfloat16)


def meet(*arrays):
    return lax.optimization_barrier(arrays)


def direct_side():
    return jnp.where(lax.axis_index("row") % 2 == 0, 3, 1)


def row_place(pair, ring, core):
    side = jnp.where(ring == direct_side(), 4 + pair * 2 + core, 9 + pair * 2 - core)
    return jnp.where(
        ring == 0, pair * 2 + core, jnp.where(ring == 2, 12 + core * 2 + pair, side)
    )


def col_place(pair, ring):
    side = jnp.where(ring == direct_side(), 2 + pair, 4 + pair)
    return jnp.where(ring == 0, pair, jnp.where(ring == 2, 6 + pair, side))


ROW_SIZES = (1, 1, 1, 1, 1, 1, 1, 1, 2, 2, 2, 2)


class Summer:
    def __init__(self, v):
        self.half = v.shape[0] // 2
        self.core = lax.axis_index("row") % 2
        self.part = v
        bits = [(p, b) for p in (0,) for b in (1, 2)]
        rings = [both_perms(lambda p, r, c, b=b: (p, r ^ b, c)) for _, b in bits]
        self.todo = [(CORE, "row"), (PAIR, "row"), (rings[0], "row"), (rings[1], "row")]
        self.todo += [(PAIR, "col"), (rings[0], "col"), (rings[1], "col")]
        self.got = over(v, *self.todo.pop(0))

    def step(self, *events):
        got, *events = meet(self.got, *events)
        self.part = self.part + got
        if len(self.todo) == 6:
            self.part = lax.dynamic_slice_in_dim(self.part, self.core * self.half, self.half, 0)
        if self.todo:
            self.got = over(self.part, *self.todo.pop(0))
        return events

    def result(self):
        other = over(self.part, CORE, "row")
        first = jnp.where(self.core == 0, self.part, other)
        second = jnp.where(self.core == 0, other, self.part)
        return jnp.concatenate([first, second], axis=0)


def gather(own, kind, extra=(), summer=None):
    step = (lambda *v: summer().step(*v)) if summer else meet
    far = over(own, PAIR, kind)
    near_a = over(own, OUT, kind)
    other = over(own, CORE, kind)
    near_b = over(other, OUT, kind)
    near_a, *extra = step(near_a, *extra)
    across = over(near_a, OUT, kind)
    near_b, _ = meet(near_b, near_a)
    across, far, _ = step(across, far, near_b)
    across_far = over(across, PAIR, kind)
    far_other = over(far, CORE, kind)
    far_a = over(far, OUT, kind)
    far_b = over(far_other, OUT, kind)
    near_b_swapped = over(near_b, CORE, kind)
    if kind == "row":
        near_a_swapped = over(near_a, CORE, kind)
        across_swapped = over(across, CORE, kind)
        far_a, _ = meet(far_a, across)
        far_a_swapped = over(far_a, CORE, kind)
    far_b, across_far = step(far_b, across_far)
    far_b_swapped = over(far_b, CORE, kind)
    if kind == "row":
        across_far_swapped = over(across_far, CORE, kind)
        pieces = [own, other, far, far_other, near_a, near_b, far_a, far_b]
        pieces += [near_a_swapped, near_b_swapped, far_a_swapped, far_b_swapped]
        pieces += [across, across_far, across_swapped, across_far_swapped]
    else:
        pieces = [own, far, near_a, far_a, near_b_swapped, far_b_swapped, across, across_far]
    return pieces, extra


def scatter(parts, kind, summer=None):
    step = (lambda *v: summer.step(*v)) if summer else meet
    parts = list(parts)
    if kind == "row":
        own, other, far, far_other, near_a, near_b, far_a, far_b = parts[:8]
        side_near, side_far, across, across_other = parts[8:]
        rows = own.shape[0]
        turned = over(across_other, CORE, kind)
        turned_far = over(side_far, CORE, kind)
        turned_near = over(side_near, CORE, kind)
        across_near = wide(across[:rows]) + wide(turned[:rows])
        across_far = narrow(wide(across[rows:]) + wide(turned[rows:]))
        far_a = narrow(wide(far_a) + wide(turned_far[:rows]))
        far_b = narrow(wide(far_b) + wide(turned_far[rows:]))
        near_a = wide(near_a) + wide(turned_near[:rows])
        near_b = narrow(wide(near_b) + wide(turned_near[rows:]))
    else:
        own, far, near_a, far_a, side_near, side_far, across_near, across_far = parts
        far_b = over(side_far, CORE, kind)
        near_b = over(side_near, CORE, kind)
        across_near, near_a = wide(across_near), wide(near_a)
        other = far_other = None

    def plus(v, w):
        return w if v is None else narrow(wide(v) + wide(w))

    got_far_b = over(far_b, BACK, kind)
    passed_far = over(across_far, PAIR, kind)
    got_far_a = over(far_a, BACK, kind)
    (got_far_b,) = step(got_far_b)
    core_far = over(plus(far_other, got_far_b), CORE, kind)
    passed_far, _ = step(passed_far, got_far_b)
    across_sum = narrow(across_near + wide(passed_far))
    passed = over(across_sum, BACK, kind)
    near_b, got_far_a, _ = meet(near_b, got_far_a, across_sum)
    got_near_b = over(near_b, BACK, kind)
    far_sum = narrow(wide(far) + wide(got_far_a) + wide(core_far))
    back_far = over(far_sum, PAIR, kind)
    passed, _ = step(passed, far_sum)
    got_near_a = over(narrow(near_a + wide(passed)), BACK, kind)
    got_near_b, _ = step(got_near_b, passed)
    core_near = over(plus(other, got_near_b), CORE, kind)
    got_near_a, back_far, core_near = meet(got_near_a, back_far, core_near)
    return wide(own) + wide(got_near_a) + wide(back_far) + wide(core_near)


def sparse_kernel(transpose, n_in, rows, cols, count, adj, *refs):
    pieces = refs[:n_in]
    outs = refs[n_in:-5]
    table, acc, blocks, piece_sem, block_sem = refs[-5:]
    piece_copies = []
    at = 0
    for i, piece in enumerate(pieces):
        part = table.at[pl.ds(at, piece.shape[0])]
        piece_copies.append(pltpu.make_async_copy(piece, part, piece_sem.at[i]))
        at += piece.shape[0]
    for copy in piece_copies:
        copy.start()
    n_chunks = count[0] // CHUNK

    def block_copy(i):
        part = pl.ds(i * CHUNK, CHUNK)
        return pltpu.make_async_copy(adj.at[part], blocks.at[part], block_sem.at[i])

    @pl.loop(0, n_chunks)
    def _(i):
        block_copy(i).start()

    @pl.loop(0, acc.shape[0] // 256)
    def _(i):
        acc[pl.ds(pl.multiple_of(i * 256, 256), 256), :] = jnp.zeros((256, acc.shape[1]), acc.dtype)

    for copy in piece_copies:
        copy.wait()

    def run(first, n):
        for slot in range(n):
            slot = first + slot
            out_at = pl.multiple_of(rows[slot] * BLK, BLK)
            in_at = pl.multiple_of(cols[slot] * BLK, BLK)
            dims = (((0,), (0,)), ((), ())) if transpose else (((1,), (0,)), ((), ()))
            acc[pl.ds(out_at, BLK), :] += lax.dot_general(
                blocks[slot],
                table[pl.ds(in_at, BLK), :],
                dims,
                preferred_element_type=jnp.float32,
            )

    n_long = n_chunks // LONG

    @pl.loop(0, n_long)
    def _(i):
        for chunk in range(LONG):
            block_copy(i * LONG + chunk).wait()
        run(i * LONG * CHUNK, LONG * CHUNK)

    @pl.loop(n_long * LONG, n_chunks)
    def _(i):
        block_copy(i).wait()
        run(i * CHUNK, CHUNK)

    at = 0
    for out in outs:

        @pl.loop(0, out.shape[0] // BLK)
        def _(j, at=at, out=out):
            here = pl.multiple_of(j * BLK, BLK)
            out[pl.ds(here, BLK), :] = acc[pl.ds(at + here, BLK), :].astype(out.dtype)

        at += out.shape[0]


def sparse(transpose, rows, cols, count, adj, pieces, sizes):
    n_in = len(pieces)
    width = pieces[0].shape[1]
    in_rows = sum(piece.shape[0] for piece in pieces)
    n_slots = adj.shape[0]
    return pl.pallas_call(
        functools.partial(sparse_kernel, transpose, n_in),
        out_shape=[jax.ShapeDtypeStruct((size, width), jnp.bfloat16) for size in sizes],
        in_specs=[pl.BlockSpec(memory_space=pltpu.SMEM)] * 3
        + [pl.BlockSpec(memory_space=pltpu.HBM)]
        + [pl.BlockSpec(memory_space=pl.ANY)] * n_in,
        out_specs=[pl.BlockSpec(memory_space=pltpu.VMEM)] * len(sizes),
        scratch_shapes=[
            pltpu.VMEM((in_rows, width), jnp.bfloat16),
            pltpu.VMEM((sum(sizes), width), jnp.float32),
            pltpu.VMEM((n_slots, BLK, BLK), jnp.bfloat16),
            pltpu.SemaphoreType.DMA((n_in,)),
            pltpu.SemaphoreType.DMA((n_slots // CHUNK,)),
        ],
        compiler_params=pltpu.CompilerParams(vmem_limit_bytes=(38 if transpose else 30) * 1024 * 1024),
        cost_estimate=pl.CostEstimate(
            flops=2 * n_slots * BLK * BLK * width,
            bytes_accessed=n_slots * BLK * BLK * 2 + (in_rows + sum(sizes)) * width * 2,
            transcendentals=0,
        ),
        name="sparse_back" if transpose else "sparse_forward",
    )(rows, cols, count, adj, *pieces)


def local(node_features, weight, bias, adj_blocks, block_row, block_col, slot_count, cotangent):
    node_rows, width = node_features.shape[2:]
    per = node_rows // BLK
    adj = adj_blocks[0, 0]
    count = slot_count[0]
    me_row = lax.axis_index("row")
    me_col = lax.axis_index("col")

    owner = block_col[0, 0] // per
    place = row_place(
        (owner // 8) ^ (me_row // 8), (owner // 2 - me_row // 2) % 4, (owner ^ me_row) % 2
    )
    in_ids = place * per + block_col[0, 0] % per
    owner = block_row[0, 0] // per
    place = col_place((owner ^ me_col) % 2, (owner // 2 - me_col // 2) % 4)
    out_ids = place * per + block_row[0, 0] % per

    pieces, (in_ids, out_ids) = gather(node_features[0, 0], "row", (in_ids, out_ids))
    sums = sparse(False, out_ids, in_ids, count, adj, pieces, [node_rows] * 8)
    aggregate = narrow(scatter(sums, "col"))

    pre = jnp.dot(aggregate, weight, preferred_element_type=jnp.float32) + bias
    sigma = jax.nn.sigmoid(pre)
    layer_out = narrow(pre * sigma)
    grad_pre = narrow(wide(cotangent[0, 0]) * sigma * (1.0 + pre * (1.0 - sigma)))

    made = []

    def summer():
        if not made:
            weight_term = lax.dot_general(
                aggregate, grad_pre, (((0,), (0,)), ((), ())), preferred_element_type=jnp.float32
            )
            bias_term = jnp.sum(wide(grad_pre), axis=0)
            spare = jnp.zeros((15, width), jnp.float32)
            made.append(Summer(jnp.concatenate([weight_term, bias_term[None], spare], axis=0)))
        return made[0]

    pieces, _ = gather(grad_pre, "col", (), summer)
    backs = sparse(
        True, in_ids, out_ids, count, adj, pieces, [node_rows * size for size in ROW_SIZES]
    )
    grad_projected = narrow(scatter(backs, "row", summer()))
    grad_input = narrow(
        lax.dot_general(
            grad_projected, weight, (((1,), (1,)), ((), ())), preferred_element_type=jnp.float32
        )
    )
    summed = summer().result()
    return (
        layer_out.reshape(1, 1, node_rows, width),
        grad_input.reshape(1, 1, node_rows, width),
        summed[:width],
        summed[width],
    )


def solution(mesh):
    placed = (
        P("col", "row", None, None),
        P(),
        P(),
        P("row", "col", None, None, None),
        P("row", "col", None),
        P("row", "col", None),
        P("row", "col"),
        P("row", "col", None, None),
    )
    return jax.shard_map(
        local,
        mesh=mesh,
        in_specs=placed,
        out_specs=(P("row", "col", None, None), P("col", "row", None, None), P(), P()),
        check_vma=False,
    )
```

```python
import functools

import jax
import jax.numpy as jnp
from jax import lax
from jax.experimental import pallas as pl
from jax.experimental.pallas import tpu as pltpu
from jax.sharding import PartitionSpec as P

BLK = 128
CHUNK = 16
LONG = 3


def both_perms(move):
    row = [
        (p * 8 + r * 2 + c, q * 8 + s * 2 + d)
        for p in range(2)
        for r in range(4)
        for c in range(2)
        for q, s, d in [move(p, r, c)]
    ]
    col = [
        (((c * 4 + r) * 2 + p), ((d * 4 + s) * 2 + q))
        for p in range(2)
        for r in range(4)
        for c in range(2)
        for q, s, d in [move(p, r, c)]
    ]
    return row, col


def over(v, perm, kind):
    if kind == "row":
        return lax.ppermute(v, "row", perm[0])
    pairs = [
        ((high * 2 + a // 8) * 8 + a % 8, (high * 2 + b // 8) * 8 + b % 8)
        for high in range(8)
        for a, b in perm[1]
    ]
    return lax.ppermute(v, ("row", "col"), pairs)


PAIR = both_perms(lambda p, r, c: (1 - p, r, c))
CORE = both_perms(lambda p, r, c: (p, r, 1 - c))
OUT = both_perms(lambda p, r, c: (p, (r + 1 - 2 * c) % 4, c))
BACK = both_perms(lambda p, r, c: (p, (r - 1 + 2 * c) % 4, c))


def wide(v):
    return v.astype(jnp.float32)


def narrow(v):
    return v.astype(jnp.bfloat16)


def meet(*arrays):
    return lax.optimization_barrier(arrays)


def direct_side():
    return jnp.where(lax.axis_index("row") % 2 == 0, 3, 1)


def row_place(pair, ring, core):
    side = jnp.where(ring == direct_side(), 4 + pair * 2 + core, 9 + pair * 2 - core)
    return jnp.where(
        ring == 0, pair * 2 + core, jnp.where(ring == 2, 12 + core * 2 + pair, side)
    )


def col_place(pair, ring):
    side = jnp.where(ring == direct_side(), 2 + pair, 4 + pair)
    return jnp.where(ring == 0, pair, jnp.where(ring == 2, 6 + pair, side))


ROW_SIZES = (1, 1, 1, 1, 1, 1, 1, 1, 2, 2, 2, 2)


class Summer:
    def __init__(self, v):
        self.half = v.shape[0] // 2
        self.core = lax.axis_index("row") % 2
        self.part = v
        bits = [(p, b) for p in (0,) for b in (1, 2)]
        rings = [both_perms(lambda p, r, c, b=b: (p, r ^ b, c)) for _, b in bits]
        self.todo = [(CORE, "row"), (PAIR, "row"), (rings[0], "row"), (rings[1], "row")]
        self.todo += [(PAIR, "col"), (rings[0], "col"), (rings[1], "col")]
        self.got = over(v, *self.todo.pop(0))

    def step(self, *events):
        got, *events = meet(self.got, *events)
        self.part = self.part + got
        if len(self.todo) == 6:
            self.part = lax.dynamic_slice_in_dim(self.part, self.core * self.half, self.half, 0)
        if self.todo:
            self.got = over(self.part, *self.todo.pop(0))
        return events

    def result(self):
        other = over(self.part, CORE, "row")
        first = jnp.where(self.core == 0, self.part, other)
        second = jnp.where(self.core == 0, other, self.part)
        return jnp.concatenate([first, second], axis=0)


def gather(own, kind, extra=(), summer=None):
    step = (lambda *v: summer().step(*v)) if summer else meet
    far = over(own, PAIR, kind)
    near_a = over(own, OUT, kind)
    other = over(own, CORE, kind)
    near_b = over(other, OUT, kind)
    near_a, *extra = step(near_a, *extra)
    across = over(near_a, OUT, kind)
    near_b, _ = meet(near_b, near_a)
    across, far, _ = step(across, far, near_b)
    across_far = over(across, PAIR, kind)
    far_other = over(far, CORE, kind)
    far_a = over(far, OUT, kind)
    far_b = over(far_other, OUT, kind)
    near_b_swapped = over(near_b, CORE, kind)
    if kind == "row":
        near_a_swapped = over(near_a, CORE, kind)
        across_swapped = over(across, CORE, kind)
        far_a, _ = meet(far_a, across)
        far_a_swapped = over(far_a, CORE, kind)
    far_b, across_far = step(far_b, across_far)
    far_b_swapped = over(far_b, CORE, kind)
    if kind == "row":
        across_far_swapped = over(across_far, CORE, kind)
        pieces = [own, other, far, far_other, near_a, near_b, far_a, far_b]
        pieces += [near_a_swapped, near_b_swapped, far_a_swapped, far_b_swapped]
        pieces += [across, across_far, across_swapped, across_far_swapped]
    else:
        pieces = [own, far, near_a, far_a, near_b_swapped, far_b_swapped, across, across_far]
    return pieces, extra


def scatter(parts, kind, summer=None):
    step = (lambda *v: summer.step(*v)) if summer else meet
    parts = list(parts)
    if kind == "row":
        own, other, far, far_other, near_a, near_b, far_a, far_b = parts[:8]
        side_near, side_far, across, across_other = parts[8:]
        rows = own.shape[0]
        turned = over(across_other, CORE, kind)
        turned_far = over(side_far, CORE, kind)
        turned_near = over(side_near, CORE, kind)
        across_near = wide(across[:rows]) + wide(turned[:rows])
        across_far = narrow(wide(across[rows:]) + wide(turned[rows:]))
        far_a = narrow(wide(far_a) + wide(turned_far[:rows]))
        far_b = narrow(wide(far_b) + wide(turned_far[rows:]))
        near_a = wide(near_a) + wide(turned_near[:rows])
        near_b = narrow(wide(near_b) + wide(turned_near[rows:]))
    else:
        own, far, near_a, far_a, side_near, side_far, across_near, across_far = parts
        far_b = over(side_far, CORE, kind)
        near_b = over(side_near, CORE, kind)
        across_near, near_a = wide(across_near), wide(near_a)
        other = far_other = None

    def plus(v, w):
        return w if v is None else narrow(wide(v) + wide(w))

    got_far_b = over(far_b, BACK, kind)
    passed_far = over(across_far, PAIR, kind)
    got_far_a = over(far_a, BACK, kind)
    if kind == "col":
        (got_far_a,) = meet(got_far_a)
        got_far_b, _ = meet(got_far_b, got_far_a)
    else:
        (got_far_b,) = step(got_far_b)
    core_far = over(plus(far_other, got_far_b), CORE, kind)
    passed_far, _ = step(passed_far, got_far_b)
    across_sum = narrow(across_near + wide(passed_far))
    passed = over(across_sum, BACK, kind)
    if kind == "row":
        near_b, got_far_a, _ = meet(near_b, got_far_a, across_sum)
    else:
        near_b, _ = meet(near_b, across_sum)
    got_near_b = over(near_b, BACK, kind)
    far_sum = narrow(wide(far) + wide(got_far_a) + wide(core_far))
    back_far = over(far_sum, PAIR, kind)
    passed, _ = step(passed, far_sum)
    got_near_a = over(narrow(near_a + wide(passed)), BACK, kind)
    got_near_b, _ = step(got_near_b, passed)
    core_near = over(plus(other, got_near_b), CORE, kind)
    got_near_a, back_far, core_near = meet(got_near_a, back_far, core_near)
    return wide(own) + wide(got_near_a) + wide(back_far) + wide(core_near)


def sparse_kernel(transpose, n_in, rows, cols, count, adj, *refs):
    pieces = refs[:n_in]
    outs = refs[n_in:-5]
    table, acc, blocks, piece_sem, block_sem = refs[-5:]
    piece_copies = []
    at = 0
    for i, piece in enumerate(pieces):
        part = table.at[pl.ds(at, piece.shape[0])]
        piece_copies.append(pltpu.make_async_copy(piece, part, piece_sem.at[i]))
        at += piece.shape[0]
    for copy in piece_copies:
        copy.start()
    n_chunks = count[0] // CHUNK

    def block_copy(i):
        part = pl.ds(i * CHUNK, CHUNK)
        return pltpu.make_async_copy(adj.at[part], blocks.at[part], block_sem.at[i])

    @pl.loop(0, n_chunks)
    def _(i):
        block_copy(i).start()

    @pl.loop(0, acc.shape[0] // 512)
    def _(i):
        here = pl.multiple_of(i * 512, 512)
        acc[pl.ds(here, 512), :] = jnp.zeros((512, acc.shape[1]), acc.dtype)

    for copy in piece_copies:
        copy.wait()

    def run(first, n):
        for slot in range(n):
            slot = first + slot
            out_at = pl.multiple_of(rows[slot] * BLK, BLK)
            in_at = pl.multiple_of(cols[slot] * BLK, BLK)
            dims = (((0,), (0,)), ((), ())) if transpose else (((1,), (0,)), ((), ()))
            acc[pl.ds(out_at, BLK), :] += lax.dot_general(
                blocks[slot],
                table[pl.ds(in_at, BLK), :],
                dims,
                preferred_element_type=jnp.float32,
            )

    n_long = n_chunks // LONG

    @pl.loop(0, n_long)
    def _(i):
        for chunk in range(LONG):
            block_copy(i * LONG + chunk).wait()
        run(i * LONG * CHUNK, LONG * CHUNK)

    @pl.loop(n_long * LONG, n_chunks)
    def _(i):
        block_copy(i).wait()
        run(i * CHUNK, CHUNK)

    at = 0
    for out in outs:

        @pl.loop(0, out.shape[0] // 1024)
        def _(j, at=at, out=out):
            here = pl.multiple_of(j * 1024, 1024)
            out[pl.ds(here, 1024), :] = acc[pl.ds(at + here, 1024), :].astype(out.dtype)

        at += out.shape[0]


def sparse(transpose, rows, cols, count, adj, pieces, sizes):
    n_in = len(pieces)
    width = pieces[0].shape[1]
    in_rows = sum(piece.shape[0] for piece in pieces)
    n_slots = adj.shape[0]
    return pl.pallas_call(
        functools.partial(sparse_kernel, transpose, n_in),
        out_shape=[jax.ShapeDtypeStruct((size, width), jnp.bfloat16) for size in sizes],
        in_specs=[pl.BlockSpec(memory_space=pltpu.SMEM)] * 3
        + [pl.BlockSpec(memory_space=pltpu.HBM)]
        + [pl.BlockSpec(memory_space=pl.ANY)] * n_in,
        out_specs=[pl.BlockSpec(memory_space=pltpu.VMEM)] * len(sizes),
        scratch_shapes=[
            pltpu.VMEM((in_rows, width), jnp.bfloat16),
            pltpu.VMEM((sum(sizes), width), jnp.float32),
            pltpu.VMEM((n_slots, BLK, BLK), jnp.bfloat16),
            pltpu.SemaphoreType.DMA((n_in,)),
            pltpu.SemaphoreType.DMA((n_slots // CHUNK,)),
        ],
        compiler_params=pltpu.CompilerParams(vmem_limit_bytes=(38 if transpose else 44) * 1024 * 1024),
        cost_estimate=pl.CostEstimate(
            flops=2 * n_slots * BLK * BLK * width,
            bytes_accessed=n_slots * BLK * BLK * 2 + (in_rows + sum(sizes)) * width * 2,
            transcendentals=0,
        ),
        name="sparse_back" if transpose else "sparse_forward",
    )(rows, cols, count, adj, *pieces)


def local(node_features, weight, bias, adj_blocks, block_row, block_col, slot_count, cotangent):
    node_rows, width = node_features.shape[2:]
    per = node_rows // BLK
    adj = adj_blocks[0, 0]
    count = slot_count[0]
    me_row = lax.axis_index("row")
    me_col = lax.axis_index("col")

    owner = block_col[0, 0] // per
    place = row_place(
        (owner // 8) ^ (me_row // 8), (owner // 2 - me_row // 2) % 4, (owner ^ me_row) % 2
    )
    in_ids = place * per + block_col[0, 0] % per
    owner = block_row[0, 0] // per
    place = col_place((owner ^ me_col) % 2, (owner // 2 - me_col // 2) % 4)
    out_ids = place * per + block_row[0, 0] % per

    pieces, (in_ids, out_ids) = gather(node_features[0, 0], "row", (in_ids, out_ids))
    sums = sparse(False, out_ids, in_ids, count, adj, pieces, [node_rows] * 8)
    aggregate = narrow(scatter(sums, "col"))

    pre = jnp.dot(aggregate, weight, preferred_element_type=jnp.float32) + bias
    sigma = jax.nn.sigmoid(pre)
    layer_out = narrow(pre * sigma)
    grad_pre = narrow(wide(cotangent[0, 0]) * sigma * (1.0 + pre * (1.0 - sigma)))

    made = []

    def summer():
        if not made:
            weight_term = lax.dot_general(
                aggregate, grad_pre, (((0,), (0,)), ((), ())), preferred_element_type=jnp.float32
            )
            bias_term = jnp.sum(wide(grad_pre), axis=0)
            spare = jnp.zeros((15, width), jnp.float32)
            made.append(Summer(jnp.concatenate([weight_term, bias_term[None], spare], axis=0)))
        return made[0]

    pieces, _ = gather(grad_pre, "col", (), summer)
    backs = sparse(
        True, in_ids, out_ids, count, adj, pieces, [node_rows * size for size in ROW_SIZES]
    )
    grad_projected = narrow(scatter(backs, "row", summer()))
    grad_input = narrow(
        lax.dot_general(
            grad_projected, weight, (((1,), (1,)), ((), ())), preferred_element_type=jnp.float32
        )
    )
    summed = summer().result()
    return (
        layer_out.reshape(1, 1, node_rows, width),
        grad_input.reshape(1, 1, node_rows, width),
        summed[:width],
        summed[width],
    )


def solution(mesh):
    placed = (
        P("col", "row", None, None),
        P(),
        P(),
        P("row", "col", None, None, None),
        P("row", "col", None),
        P("row", "col", None),
        P("row", "col"),
        P("row", "col", None, None),
    )
    return jax.shard_map(
        local,
        mesh=mesh,
        in_specs=placed,
        out_specs=(P("row", "col", None, None), P("col", "row", None, None), P(), P()),
        check_vma=False,
    )
```

```python
import functools

import jax
import jax.numpy as jnp
from jax import lax
from jax.experimental import pallas as pl
from jax.experimental.pallas import tpu as pltpu
from jax.sharding import PartitionSpec as P

BLK = 128
CHUNK = 16
LONG = 3


def both_perms(move):
    row = [
        (p * 8 + r * 2 + c, q * 8 + s * 2 + d)
        for p in range(2)
        for r in range(4)
        for c in range(2)
        for q, s, d in [move(p, r, c)]
    ]
    col = [
        (((c * 4 + r) * 2 + p), ((d * 4 + s) * 2 + q))
        for p in range(2)
        for r in range(4)
        for c in range(2)
        for q, s, d in [move(p, r, c)]
    ]
    return row, col


def over(v, perm, kind):
    if kind == "row":
        return lax.ppermute(v, "row", perm[0])
    pairs = [
        ((high * 2 + a // 8) * 8 + a % 8, (high * 2 + b // 8) * 8 + b % 8)
        for high in range(8)
        for a, b in perm[1]
    ]
    return lax.ppermute(v, ("row", "col"), pairs)


PAIR = both_perms(lambda p, r, c: (1 - p, r, c))
CORE = both_perms(lambda p, r, c: (p, r, 1 - c))
OUT = both_perms(lambda p, r, c: (p, (r + 1 - 2 * c) % 4, c))
BACK = both_perms(lambda p, r, c: (p, (r - 1 + 2 * c) % 4, c))


def wide(v):
    return v.astype(jnp.float32)


def narrow(v):
    return v.astype(jnp.bfloat16)


def meet(*arrays):
    return lax.optimization_barrier(arrays)


def direct_side():
    return jnp.where(lax.axis_index("row") % 2 == 0, 3, 1)


def row_place(pair, ring, core):
    side = jnp.where(ring == direct_side(), 4 + pair * 2 + core, 9 + pair * 2 - core)
    return jnp.where(
        ring == 0, pair * 2 + core, jnp.where(ring == 2, 12 + core * 2 + pair, side)
    )


def col_place(pair, ring):
    side = jnp.where(ring == direct_side(), 2 + pair, 4 + pair)
    return jnp.where(ring == 0, pair, jnp.where(ring == 2, 6 + pair, side))


ROW_SIZES = (1, 1, 1, 1, 1, 1, 1, 1, 2, 2, 2, 2)


class Summer:
    def __init__(self, v):
        self.half = v.shape[0] // 2
        self.core = lax.axis_index("row") % 2
        self.part = v
        bits = [(p, b) for p in (0,) for b in (1, 2)]
        rings = [both_perms(lambda p, r, c, b=b: (p, r ^ b, c)) for _, b in bits]
        self.todo = [(CORE, "row"), (PAIR, "row"), (rings[0], "row"), (rings[1], "row")]
        self.todo += [(PAIR, "col"), (rings[0], "col"), (rings[1], "col")]
        self.got = over(v, *self.todo.pop(0))

    def step(self, *events):
        got, *events = meet(self.got, *events)
        self.part = self.part + got
        if len(self.todo) == 6:
            self.part = lax.dynamic_slice_in_dim(self.part, self.core * self.half, self.half, 0)
        if self.todo:
            self.got = over(self.part, *self.todo.pop(0))
        return events

    def result(self):
        other = over(self.part, CORE, "row")
        first = jnp.where(self.core == 0, self.part, other)
        second = jnp.where(self.core == 0, other, self.part)
        return jnp.concatenate([first, second], axis=0)


def gather(own, kind, extra=(), summer=None):
    step = (lambda *v: summer().step(*v)) if summer else meet
    far = over(own, PAIR, kind)
    near_a = over(own, OUT, kind)
    other = over(own, CORE, kind)
    near_b = over(other, OUT, kind)
    (near_a,) = step(near_a)
    across = over(near_a, OUT, kind)
    near_b, _ = meet(near_b, near_a)
    across, far, _, *extra = step(across, far, near_b, *extra)
    across_far = over(across, PAIR, kind)
    far_other = over(far, CORE, kind)
    far_a = over(far, OUT, kind)
    far_b = over(far_other, OUT, kind)
    near_b_swapped = over(near_b, CORE, kind)
    if kind == "row":
        near_a_swapped = over(near_a, CORE, kind)
        across_swapped = over(across, CORE, kind)
        far_a, _ = meet(far_a, across)
        far_a_swapped = over(far_a, CORE, kind)
    far_b, across_far = step(far_b, across_far)
    far_b_swapped = over(far_b, CORE, kind)
    if kind == "row":
        across_far_swapped = over(across_far, CORE, kind)
        pieces = [own, other, far, far_other, near_a, near_b, far_a, far_b]
        pieces += [near_a_swapped, near_b_swapped, far_a_swapped, far_b_swapped]
        pieces += [across, across_far, across_swapped, across_far_swapped]
    else:
        pieces = [own, far, near_a, far_a, near_b_swapped, far_b_swapped, across, across_far]
    return pieces, extra


def scatter(parts, kind, summer=None):
    step = (lambda *v: summer.step(*v)) if summer else meet
    parts = list(parts)
    if kind == "row":
        own, other, far, far_other, near_a, near_b, far_a, far_b = parts[:8]
        side_near, side_far, across, across_other = parts[8:]
        rows = own.shape[0]
        turned = over(across_other, CORE, kind)
        turned_far = over(side_far, CORE, kind)
        turned_near = over(side_near, CORE, kind)
        across_near = wide(across[:rows]) + wide(turned[:rows])
        across_far = narrow(wide(across[rows:]) + wide(turned[rows:]))
        far_a = narrow(wide(far_a) + wide(turned_far[:rows]))
        far_b = narrow(wide(far_b) + wide(turned_far[rows:]))
        near_a = wide(near_a) + wide(turned_near[:rows])
        near_b = narrow(wide(near_b) + wide(turned_near[rows:]))
    else:
        own, far, near_a, far_a, side_near, side_far, across_near, across_far = parts
        far_b = over(side_far, CORE, kind)
        near_b = over(side_near, CORE, kind)
        across_near, near_a = wide(across_near), wide(near_a)
        other = far_other = None

    def plus(v, w):
        return w if v is None else narrow(wide(v) + wide(w))

    got_far_b = over(far_b, BACK, kind)
    passed_far = over(across_far, PAIR, kind)
    got_far_a = over(far_a, BACK, kind)
    if kind == "col":
        (got_far_a,) = meet(got_far_a)
        got_far_b, _ = meet(got_far_b, got_far_a)
    else:
        (got_far_b,) = step(got_far_b)
    core_far = over(plus(far_other, got_far_b), CORE, kind)
    passed_far, _ = step(passed_far, got_far_b)
    across_sum = narrow(across_near + wide(passed_far))
    passed = over(across_sum, BACK, kind)
    if kind == "row":
        near_b, got_far_a, _ = meet(near_b, got_far_a, across_sum)
    else:
        near_b, _ = meet(near_b, across_sum)
    got_near_b = over(near_b, BACK, kind)
    far_sum = narrow(wide(far) + wide(got_far_a) + wide(core_far))
    back_far = over(far_sum, PAIR, kind)
    passed, _ = step(passed, far_sum)
    got_near_a = over(narrow(near_a + wide(passed)), BACK, kind)
    got_near_b, _ = step(got_near_b, passed)
    core_near = over(plus(other, got_near_b), CORE, kind)
    got_near_a, back_far, core_near = meet(got_near_a, back_far, core_near)
    return wide(own) + wide(got_near_a) + wide(back_far) + wide(core_near)


def sparse_kernel(transpose, n_in, rows, cols, count, adj, *refs):
    pieces = refs[:n_in]
    outs = refs[n_in:-5]
    table, acc, blocks, piece_sem, block_sem = refs[-5:]
    piece_copies = []
    at = 0
    for i, piece in enumerate(pieces):
        part = table.at[pl.ds(at, piece.shape[0])]
        piece_copies.append(pltpu.make_async_copy(piece, part, piece_sem.at[i]))
        at += piece.shape[0]
    for copy in piece_copies:
        copy.start()
    n_chunks = count[0] // CHUNK

    def block_copy(i):
        part = pl.ds(i * CHUNK, CHUNK)
        return pltpu.make_async_copy(adj.at[part], blocks.at[part], block_sem.at[i])

    @pl.loop(0, n_chunks)
    def _(i):
        block_copy(i).start()

    @pl.loop(0, acc.shape[0] // 512)
    def _(i):
        here = pl.multiple_of(i * 512, 512)
        acc[pl.ds(here, 512), :] = jnp.zeros((512, acc.shape[1]), acc.dtype)

    for copy in piece_copies:
        copy.wait()

    def run(first, n):
        for slot in range(n):
            slot = first + slot
            out_at = pl.multiple_of(rows[slot] * BLK, BLK)
            in_at = pl.multiple_of(cols[slot] * BLK, BLK)
            dims = (((0,), (0,)), ((), ())) if transpose else (((1,), (0,)), ((), ()))
            acc[pl.ds(out_at, BLK), :] += lax.dot_general(
                blocks[slot],
                table[pl.ds(in_at, BLK), :],
                dims,
                preferred_element_type=jnp.float32,
            )

    n_long = n_chunks // LONG

    @pl.loop(0, n_long)
    def _(i):
        for chunk in range(LONG):
            block_copy(i * LONG + chunk).wait()
        run(i * LONG * CHUNK, LONG * CHUNK)

    @pl.loop(n_long * LONG, n_chunks)
    def _(i):
        block_copy(i).wait()
        run(i * CHUNK, CHUNK)

    at = 0
    for out in outs:

        @pl.loop(0, out.shape[0] // 1024)
        def _(j, at=at, out=out):
            here = pl.multiple_of(j * 1024, 1024)
            out[pl.ds(here, 1024), :] = acc[pl.ds(at + here, 1024), :].astype(out.dtype)

        at += out.shape[0]


def sparse(transpose, rows, cols, count, adj, pieces, sizes):
    n_in = len(pieces)
    width = pieces[0].shape[1]
    in_rows = sum(piece.shape[0] for piece in pieces)
    n_slots = adj.shape[0]
    return pl.pallas_call(
        functools.partial(sparse_kernel, transpose, n_in),
        out_shape=[jax.ShapeDtypeStruct((size, width), jnp.bfloat16) for size in sizes],
        in_specs=[pl.BlockSpec(memory_space=pltpu.SMEM)] * 3
        + [pl.BlockSpec(memory_space=pltpu.HBM)]
        + [pl.BlockSpec(memory_space=pl.ANY)] * n_in,
        out_specs=[pl.BlockSpec(memory_space=pltpu.VMEM)] * len(sizes),
        scratch_shapes=[
            pltpu.VMEM((in_rows, width), jnp.bfloat16),
            pltpu.VMEM((sum(sizes), width), jnp.float32),
            pltpu.VMEM((n_slots, BLK, BLK), jnp.bfloat16),
            pltpu.SemaphoreType.DMA((n_in,)),
            pltpu.SemaphoreType.DMA((n_slots // CHUNK,)),
        ],
        compiler_params=pltpu.CompilerParams(vmem_limit_bytes=(38 if transpose else 44) * 1024 * 1024),
        cost_estimate=pl.CostEstimate(
            flops=2 * n_slots * BLK * BLK * width,
            bytes_accessed=n_slots * BLK * BLK * 2 + (in_rows + sum(sizes)) * width * 2,
            transcendentals=0,
        ),
        name="sparse_back" if transpose else "sparse_forward",
    )(rows, cols, count, adj, *pieces)


def local(node_features, weight, bias, adj_blocks, block_row, block_col, slot_count, cotangent):
    node_rows, width = node_features.shape[2:]
    per = node_rows // BLK
    adj = adj_blocks[0, 0]
    count = slot_count[0]
    me_row = lax.axis_index("row")
    me_col = lax.axis_index("col")

    owner = block_col[0, 0] // per
    place = row_place(
        (owner // 8) ^ (me_row // 8), (owner // 2 - me_row // 2) % 4, (owner ^ me_row) % 2
    )
    in_ids = place * per + block_col[0, 0] % per
    owner = block_row[0, 0] // per
    place = col_place((owner ^ me_col) % 2, (owner // 2 - me_col // 2) % 4)
    out_ids = place * per + block_row[0, 0] % per

    pieces, (in_ids, out_ids) = gather(node_features[0, 0], "row", (in_ids, out_ids))
    sums = sparse(False, out_ids, in_ids, count, adj, pieces, [node_rows] * 8)
    aggregate = narrow(scatter(sums, "col"))

    pre = jnp.dot(aggregate, weight, preferred_element_type=jnp.float32) + bias
    sigma = jax.nn.sigmoid(pre)
    layer_out = narrow(pre * sigma)
    grad_pre = narrow(wide(cotangent[0, 0]) * sigma * (1.0 + pre * (1.0 - sigma)))

    made = []

    def summer():
        if not made:
            weight_term = lax.dot_general(
                aggregate, grad_pre, (((0,), (0,)), ((), ())), preferred_element_type=jnp.float32
            )
            bias_term = jnp.sum(wide(grad_pre), axis=0)
            spare = jnp.zeros((15, width), jnp.float32)
            made.append(Summer(jnp.concatenate([weight_term, bias_term[None], spare], axis=0)))
        return made[0]

    pieces, _ = gather(grad_pre, "col", (), summer)
    backs = sparse(
        True, in_ids, out_ids, count, adj, pieces, [node_rows * size for size in ROW_SIZES]
    )
    grad_projected = narrow(scatter(backs, "row", summer()))
    grad_input = narrow(
        lax.dot_general(
            grad_projected, weight, (((1,), (1,)), ((), ())), preferred_element_type=jnp.float32
        )
    )
    summed = summer().result()
    return (
        layer_out.reshape(1, 1, node_rows, width),
        grad_input.reshape(1, 1, node_rows, width),
        summed[:width],
        summed[width],
    )


def solution(mesh):
    placed = (
        P("col", "row", None, None),
        P(),
        P(),
        P("row", "col", None, None, None),
        P("row", "col", None),
        P("row", "col", None),
        P("row", "col"),
        P("row", "col", None, None),
    )
    return jax.shard_map(
        local,
        mesh=mesh,
        in_specs=placed,
        out_specs=(P("row", "col", None, None), P("col", "row", None, None), P(), P()),
        check_vma=False,
    )
```
